32 devices in a mesh: groups: 2 (over y), sec: 4 (over z), term: 4 (over x, core).
Axes of the slice: x: 2, y: 2, z: 4, core: 2. Of those that a mesh axis runs over, the one named last changes fastest.
Arguments:
- wavefunction: bfloat16 [256, 3, 128, 128], P(('groups', 'sec')), parts along dimension 0, may hold values from -6 to 6
- left_ops: bfloat16 [256, 16, 128, 128], P(('groups', 'sec'), 'term'), parts along dimension 0, may hold values from -0.5 to 0.5
- right_ops: bfloat16 [256, 16, 128, 128], P(('groups', 'sec'), 'term'), parts along dimension 0, may hold values from -0.125 to 0.125
- sector_sizes: int32 [256], P('groups'), parts along dimension 0, may hold values from 16 to 128
- right_partner: int32 [256], P('groups'), parts along dimension 0, may hold values from 0 to 127, as said below
Outputs:
- sigma_blocks: float32 [256, 3, 128, 128], P(('groups', 'sec', 'term')), parts along dimension 0
The draws below stay inside these ranges and needn't reach their ends.
There are 2 independent parts, one for each index of `groups`. The reference program is written for one: setup_inputs(seed, part) draws one part's arguments, and reference() takes and returns one part's arrays. A program takes and returns all parts, laid end to end along the dimension named above; each array names one. Nothing has to cross between parts.
Inputs may be any that keep to these rules, and one draw needn't show every extreme that they name: `right_partner`: a permutation of the 128 sectors; the 32 sectors of one device of sec have partners on at most 8 sectors of any one device, and this number is reached.
All inputs are finite; a program needn't handle non-finite values.
Results may differ from the reference program's by a relative error of at most 0.003.
Values may be sent and summed in bfloat16 or wider, within the bound.
A program may use at most 128 MiB of HBM per device.

```python
import jax
import jax.numpy as jnp
from jax import lax

BLOCK = 128
VECS = 3
S_DEV = 32
SECTORS = 128
TERMS = 16
N_SEC = 4


def draw_right_partner(key, part):
    key = jax.random.fold_in(key, 11)
    keys = jax.random.split(key, 4)
    device_order = jax.random.permutation(keys[0], N_SEC)
    inverse_order = jnp.argsort(device_order)
    offsets = jax.random.permutation(keys[1], N_SEC)[jnp.arange(S_DEV) % N_SEC]
    offsets = jax.random.permutation(keys[2], offsets)
    landing = jax.random.permutation(keys[3], S_DEV)
    sector_ids = jnp.arange(SECTORS)
    owner_dev = sector_ids // S_DEV
    within = sector_ids % S_DEV
    target = device_order[(inverse_order[owner_dev] + offsets[within]) % N_SEC]
    return (target * S_DEV + landing[within]).astype(jnp.int32)


def plant(array, key, low, top_value):
    longest = array.shape.index(max(array.shape))
    spots = []
    for shift in (0, 1):
        where = [jax.random.randint(jax.random.fold_in(key, axis), (), 0, length) for axis, length in enumerate(array.shape)]
        where[longest] = (where[longest] + shift) % array.shape[longest]
        spots.append(tuple(where))
    return array.at[spots[0]].set(low).at[spots[1]].set(top_value)


def levels(key, dims, cuts, smallest, high):
    loudness = 1.0
    for position, shards_of in cuts:
        draws = jax.random.uniform(jax.random.fold_in(jax.random.fold_in(key, 6), position), (shards_of,), jnp.float32, smallest / len(cuts), high / len(cuts))
        loudness = loudness * jnp.repeat(jnp.exp(draws), dims[position] // shards_of).reshape((-1,) + (1,) * (len(dims) - 1 - position))
    return loudness


def scatter_about(rng, extent, deviation, bound, cuts=(), held_as=jnp.bfloat16):
    entries = jax.random.normal(rng, extent, jnp.float32) * deviation
    if len(cuts) > 0:
        entries = levels(rng, extent, cuts, -0.22, 0.18) * entries
    return jnp.clip(entries, min=-bound, max=bound).astype(held_as)


def setup_inputs(seed: int = 0, part: int = 0) -> dict:
    key_of = jax.random.split(jax.random.key(seed), 6)
    part_splits = jax.random.split(jax.random.fold_in(key_of[5], part), 6)
    wavefunction = scatter_about(part_splits[0], (SECTORS, VECS, BLOCK, BLOCK), 1.0, 6.0, ((0, 4),))
    left_ops = scatter_about(part_splits[1], (SECTORS, TERMS, BLOCK, BLOCK), BLOCK ** -0.5, 0.5, ((0, 4), (1, 4)))
    right_ops = scatter_about(part_splits[2], (SECTORS, TERMS, BLOCK, BLOCK), (BLOCK * TERMS) ** -0.5, 0.125, ((0, 4), (1, 4)))
    sector_sizes = plant(jax.random.randint(part_splits[3], (SECTORS,), BLOCK // 8, BLOCK + 1), jax.random.fold_in(part_splits[3], 1), BLOCK // 8, BLOCK).astype(jnp.int32)
    right_partner = draw_right_partner(jax.random.fold_in(jax.random.fold_in(key_of[5], part), 71), part)
    return {"wavefunction": wavefunction, "left_ops": left_ops, "right_ops": right_ops, "sector_sizes": sector_sizes, "right_partner": right_partner}


def reference(wavefunction, left_ops, right_ops, sector_sizes, right_partner):
    row_ids = jnp.arange(BLOCK, dtype=jnp.int32)
    left_keep = (row_ids[None, :] < sector_sizes[:, None]).astype(jnp.float32)
    right_sizes = sector_sizes[right_partner]
    right_keep = (row_ids[None, :] < right_sizes[:, None]).astype(jnp.float32)
    keep = left_keep[:, None, :, None] * right_keep[:, None, None, :]
    masked = jnp.where(keep > 0, wavefunction, jnp.zeros_like(wavefunction))
    masked_wide = masked.astype(jnp.float32)
    right_paired = right_ops[right_partner]

    def one_term(running, term_index):
        left_block = left_ops[:, term_index].astype(jnp.float32)
        partial_value = jnp.einsum('sij,svjk->svik', left_block, masked_wide).astype(jnp.bfloat16)
        right_block = right_paired[:, term_index].astype(jnp.float32)
        return running + jnp.einsum('svik,smk->svim', partial_value.astype(jnp.float32), right_block), None

    start = jnp.zeros((SECTORS, VECS, BLOCK, BLOCK), jnp.float32)
    summed, unused = lax.scan(one_term, start, jnp.arange(TERMS, dtype=jnp.int32))
    return summed * keep
```

```python
import functools

import jax
import jax.numpy as jnp
from jax import lax
from jax.experimental import pallas as pl
from jax.experimental.pallas import tpu as pltpu
from jax.sharding import PartitionSpec as P

MESH = pl.DeviceIdType.MESH
CHUNKS = (32, 32, 32, 16, 16)
AHEAD = 2


def kernel(chunks, receive_index, slot_of, sizes, partner, wave_hbm, left_hbm, right_hbm, out_ref,
           wave, left, right, partial, *rest):
    n_chunks = len(chunks)
    outgoing, arrived, sums, landed = (rest[i * n_chunks:(i + 1) * n_chunks] for i in range(4))
    load_sem, send_sem, recv_sem, sum_send_sem, sum_recv_sem = rest[4 * n_chunks:]
    sector_count, vecs, block, _ = wave.shape
    terms = left.shape[1]
    peers = lax.axis_size("sec")
    owners = lax.axis_size("term")
    capacity = sector_count // peers
    owned = sector_count // owners
    me = lax.axis_index("sec")
    my_term = lax.axis_index("term")
    starts = [sum(chunks[:c]) for c in range(n_chunks)]

    right_load = pltpu.make_async_copy(right_hbm, right, load_sem.at[0])
    left_load = pltpu.make_async_copy(left_hbm, left, load_sem.at[1])
    wave_load = pltpu.make_async_copy(wave_hbm, wave, load_sem.at[2])
    right_load.start()
    left_load.start()
    wave_load.start()

    barrier = pltpu.get_barrier_semaphore()

    def greet_sec(i, carry):
        pl.semaphore_signal(barrier, inc=1, device_id={"sec": lax.rem(me + i, peers)}, device_id_type=MESH)
        return carry

    def greet_term(i, carry):
        pl.semaphore_signal(barrier, inc=1, device_id={"term": lax.rem(my_term + i, owners)}, device_id_type=MESH)
        return carry

    lax.fori_loop(1, peers, greet_sec, 0)
    lax.fori_loop(1, owners, greet_term, 0)
    right_load.wait()

    def pick(c, target, into, slot_base):
        def one(r, carry):
            index = receive_index[target * capacity + r]
            for t in range(terms):
                into[slot_base + r, :, t * block:(t + 1) * block] = right[index, t, starts[c]:starts[c] + chunks[c], :]
            return carry
        lax.fori_loop(0, capacity, one, 0)

    def block_copy(c, target):
        return pltpu.make_async_remote_copy(
            src_ref=outgoing[c].at[pl.ds(target * capacity, capacity)],
            dst_ref=arrived[c].at[pl.ds(me * capacity, capacity)],
            send_sem=send_sem.at[c, target],
            recv_sem=recv_sem.at[c, me],
            device_id={"sec": target},
            device_id_type=MESH,
        )

    def arrival(c, source):
        return pltpu.make_async_remote_copy(
            src_ref=outgoing[c].at[pl.ds(source * capacity, capacity)],
            dst_ref=arrived[c].at[pl.ds(source * capacity, capacity)],
            send_sem=send_sem.at[c, source],
            recv_sem=recv_sem.at[c, source],
            device_id={"sec": source},
            device_id_type=MESH,
        )

    def far_first(i):
        return lax.rem(me + 1 + lax.rem(i + peers // 2 - 1, peers - 1), peers)

    def launch(c):
        def one(i, carry):
            target = far_first(i)
            pick(c, target, outgoing[c], target * capacity)
            block_copy(c, target).start()
            return carry
        lax.fori_loop(0, peers - 1, one, 0)

    def sent(c):
        def one(i, carry):
            block_copy(c, far_first(i)).wait_send()
            return carry
        lax.fori_loop(0, peers - 1, one, 0)

    def arrive(c):
        def one(i, carry):
            arrival(c, far_first(i)).wait_recv()
            return carry
        lax.fori_loop(0, peers - 1, one, 0)

    def sum_copy(c, owner):
        return pltpu.make_async_remote_copy(
            src_ref=sums[c].at[owner],
            dst_ref=landed[c].at[my_term],
            send_sem=sum_send_sem.at[c, owner],
            recv_sem=sum_recv_sem.at[c, my_term],
            device_id={"term": owner},
            device_id_type=MESH,
        )

    def sum_arrival(c, source):
        return pltpu.make_async_remote_copy(
            src_ref=sums[c].at[source],
            dst_ref=landed[c].at[source],
            send_sem=sum_send_sem.at[c, source],
            recv_sem=sum_recv_sem.at[c, source],
            device_id={"term": source},
            device_id_type=MESH,
        )

    pl.semaphore_wait(barrier, peers - 1 + owners - 1)
    for c in range(min(AHEAD, n_chunks)):
        launch(c)
    for c in range(n_chunks):
        pick(c, me, arrived[c], me * capacity)

    left_load.wait()
    wave_load.wait()
    row_ids = lax.broadcasted_iota(jnp.int32, (block, block), 0)
    column_ids = lax.broadcasted_iota(jnp.int32, (block, block), 1)

    def first_products(l, carry):
        own_size = sizes[me * sector_count + l]
        right_size = sizes[partner[me * sector_count + l]]
        keep = (row_ids < own_size) & (column_ids < right_size)
        masked = jnp.concatenate(
            [jnp.where(keep, wave[l, v].astype(jnp.float32), 0.0).astype(jnp.bfloat16) for v in range(vecs)], axis=1
        )
        for t in range(terms):
            product = jnp.dot(left[l, t], masked, preferred_element_type=jnp.float32).astype(jnp.bfloat16)
            for v in range(vecs):
                partial[l, v * block:(v + 1) * block, t * block:(t + 1) * block] = product[:, v * block:(v + 1) * block]
        return carry

    lax.fori_loop(0, sector_count, first_products, 0)

    def second_product(c, l):
        return lax.dot_general(
            arrived[c][slot_of[l]], partial[l], (((1,), (1,)), ((), ())), preferred_element_type=jnp.float32
        )

    def finish(c):
        rows = pl.ds(starts[c], chunks[c])

        def wait_one(i, carry):
            sum_arrival(c, lax.rem(my_term + i, owners)).wait_recv()
            return carry
        lax.fori_loop(1, owners, wait_one, 0)

        def add(s, carry):
            total = out_ref[s, rows, :]
            for i in range(1, owners):
                total = total + landed[c][lax.rem(my_term + i, owners), s].astype(jnp.float32)
            out_ref[s, rows, :] = total
            return carry
        lax.fori_loop(0, owned, add, 0)

    for c in range(n_chunks):
        arrive(c)
        if c + AHEAD < n_chunks:
            launch(c + AHEAD)

        def for_owner(i, carry):
            owner = lax.rem(my_term + i, owners)

            def one(s, inner):
                sums[c][owner, s] = second_product(c, owner * owned + s).astype(jnp.bfloat16)
                return inner
            lax.fori_loop(0, owned, one, 0)
            sum_copy(c, owner).start()
            return carry
        lax.fori_loop(1, owners, for_owner, 0)

        def for_me(s, carry):
            out_ref[s, starts[c]:starts[c] + chunks[c], :] = second_product(c, my_term * owned + s)
            return carry
        lax.fori_loop(0, owned, for_me, 0)
        if c > 0:
            finish(c - 1)
    finish(n_chunks - 1)

    for c in range(n_chunks):
        sent(c)

        def sum_sent(i, carry):
            sum_copy(c, lax.rem(my_term + i, owners)).wait_send()
            return carry
        lax.fori_loop(1, owners, sum_sent, 0)


def on_device(wavefunction, left_ops, right_ops, sector_sizes, right_partner):
    sector_count, vecs, block = wavefunction.shape[:3]
    terms = left_ops.shape[1]
    peers = lax.axis_size("sec")
    owners = lax.axis_size("term")
    own_index = lax.axis_index("sec")
    term_index = lax.axis_index("term")
    capacity = sector_count // peers
    owned = sector_count // owners
    sector_ids = jnp.arange(sector_sizes.shape[0], dtype=jnp.int32)
    source_dev = sector_ids // sector_count
    target_dev = right_partner // sector_count
    earlier = (
        (source_dev[:, None] == source_dev[None, :])
        & (target_dev[:, None] == target_dev[None, :])
        & (sector_ids[None, :] < sector_ids[:, None])
    )
    rank_within = jnp.sum(earlier.astype(jnp.int32), axis=1)
    slot_of = target_dev * capacity + rank_within
    local_slot = lax.dynamic_slice_in_dim(slot_of, own_index * sector_count, sector_count)
    slot_range = jnp.arange(sector_count, dtype=jnp.int32)
    receive_key = jnp.where(target_dev == own_index, source_dev * capacity + rank_within, -1)
    receive_index = jnp.sum(
        jnp.where(receive_key[None, :] == slot_range[:, None], (right_partner % sector_count)[None, :], 0), axis=1
    )

    chunks = CHUNKS
    wide = terms * block
    columns = vecs * block
    n = len(chunks)
    vmem = lambda shape, dtype: pltpu.VMEM(shape, dtype)
    scratch = [
        vmem(wavefunction.shape, jnp.bfloat16),
        vmem(left_ops.shape, jnp.bfloat16),
        vmem(right_ops.shape, jnp.bfloat16),
        vmem((sector_count, columns, wide), jnp.bfloat16),
    ]
    scratch += [vmem((sector_count, rows, wide), jnp.bfloat16) for rows in chunks]
    scratch += [vmem((sector_count, rows, wide), jnp.bfloat16) for rows in chunks]
    scratch += [vmem((owners, owned, rows, columns), jnp.bfloat16) for rows in chunks]
    scratch += [vmem((owners, owned, rows, columns), jnp.bfloat16) for rows in chunks]
    scratch += [
        pltpu.SemaphoreType.DMA((3,)),
        pltpu.SemaphoreType.DMA((n, peers)),
        pltpu.SemaphoreType.DMA((n, peers)),
        pltpu.SemaphoreType.DMA((n, owners)),
        pltpu.SemaphoreType.DMA((n, owners)),
    ]
    smem = pl.BlockSpec(memory_space=pltpu.SMEM)
    anywhere = pl.BlockSpec(memory_space=pl.ANY)
    summed = pl.pallas_call(
        functools.partial(kernel, chunks),
        out_shape=jax.ShapeDtypeStruct((owned, block, columns), jnp.float32),
        in_specs=[smem, smem, smem, smem, anywhere, anywhere, anywhere],
        out_specs=pl.BlockSpec(memory_space=pltpu.VMEM),
        scratch_shapes=scratch,
        compiler_params=pltpu.CompilerParams(
            collective_id=0, has_side_effects=True, vmem_limit_bytes=52 * 1024 * 1024
        ),
        cost_estimate=pl.CostEstimate(
            flops=4 * sector_count * terms * vecs * block**3, bytes_accessed=16 * 1024 * 1024, transcendentals=0
        ),
    )(receive_index, local_slot, sector_sizes, right_partner, wavefunction, left_ops, right_ops)

    first = own_index * sector_count + term_index * owned
    own_sizes = lax.dynamic_slice_in_dim(sector_sizes, first, owned)
    own_partner = lax.dynamic_slice_in_dim(right_partner, first, owned)
    right_sizes = jnp.sum(jnp.where(own_partner[:, None] == sector_ids[None, :], sector_sizes[None, :], 0), axis=1)
    row_ids = jnp.arange(block, dtype=jnp.int32)
    keep = (row_ids[None, :] < own_sizes[:, None])[:, :, None] & (row_ids[None, :] < right_sizes[:, None])[:, None, :]
    sigma = summed.reshape(owned, block, vecs, block).transpose(0, 2, 3, 1)
    return jnp.where(keep[:, None], sigma, jnp.zeros_like(sigma))


def solution(mesh):
    placed = (
        P(("groups", "sec"), None, None, None),
        P(("groups", "sec"), "term", None, None),
        P(("groups", "sec"), "term", None, None),
        P("groups"),
        P("groups"),
    )
    return jax.shard_map(
        on_device,
        mesh=mesh,
        in_specs=placed,
        out_specs=P(("groups", "sec", "term"), None, None, None),
        check_vma=False,
    )
```

```python
import functools

import jax
import jax.numpy as jnp
from jax import lax
from jax.experimental import pallas as pl
from jax.experimental.pallas import tpu as pltpu
from jax.sharding import PartitionSpec as P

MESH = pl.DeviceIdType.MESH
CHUNKS = (48, 32, 32, 16)


def kernel(chunks, receive_index, slot_of, sector_of, sizes_hbm, partner_hbm, wave_hbm, left_hbm, right_hbm, out_ref,
           sizes, partner, wave, left, partial, products, *rest):
    n_chunks = len(chunks)
    right, outgoing, arrived, sums, landed = (rest[i * n_chunks:(i + 1) * n_chunks] for i in range(5))
    load_sem, send_sem, recv_sem, sum_send_sem, sum_recv_sem = rest[5 * n_chunks:]
    sector_count, vecs, block, _ = wave.shape
    terms = left.shape[1]
    peers = lax.axis_size("sec")
    owners = lax.axis_size("term")
    capacity = sector_count // peers
    owned = sector_count // owners
    me = lax.axis_index("sec")
    my_term = lax.axis_index("term")
    starts = [sum(chunks[:c]) for c in range(n_chunks)]

    right_loads = [
        pltpu.make_async_copy(right_hbm.at[:, :, pl.ds(starts[c], chunks[c])], right[c], load_sem.at[4 + c])
        for c in range(n_chunks)
    ]
    left_load = pltpu.make_async_copy(left_hbm, left, load_sem.at[0])
    wave_load = pltpu.make_async_copy(wave_hbm, wave, load_sem.at[1])
    sizes_load = pltpu.make_async_copy(sizes_hbm, sizes, load_sem.at[2])
    partner_load = pltpu.make_async_copy(partner_hbm, partner, load_sem.at[3])
    for load in right_loads:
        load.start()

    barrier = pltpu.get_barrier_semaphore()

    def greet_sec(i, carry):
        pl.semaphore_signal(barrier, inc=1, device_id={"sec": lax.rem(me + i, peers)}, device_id_type=MESH)
        return carry

    def greet_term(i, carry):
        pl.semaphore_signal(barrier, inc=1, device_id={"term": lax.rem(my_term + i, owners)}, device_id_type=MESH)
        return carry

    lax.fori_loop(1, peers, greet_sec, 0)
    lax.fori_loop(1, owners, greet_term, 0)
    def pick(c, target, into, slot_base):
        def one(r, carry):
            index = receive_index[target * capacity + r]
            for t in range(terms):
                into[slot_base + r, :, t * block:(t + 1) * block] = right[c][index, t]
            return carry
        lax.fori_loop(0, capacity, one, 0, unroll=min(capacity, 4))

    def block_copy(c, target):
        return pltpu.make_async_remote_copy(
            src_ref=outgoing[c].at[pl.ds(target * capacity, capacity)],
            dst_ref=arrived[c].at[pl.ds(me * capacity, capacity)],
            send_sem=send_sem.at[c, target],
            recv_sem=recv_sem.at[c, me],
            device_id={"sec": target},
            device_id_type=MESH,
        )

    def arrival(c, source):
        return pltpu.make_async_remote_copy(
            src_ref=outgoing[c].at[pl.ds(source * capacity, capacity)],
            dst_ref=arrived[c].at[pl.ds(source * capacity, capacity)],
            send_sem=send_sem.at[c, source],
            recv_sem=recv_sem.at[c, source],
            device_id={"sec": source},
            device_id_type=MESH,
        )

    def others(i, index, count):
        base = index - lax.rem(index, 2)
        far = lax.rem(base + 2 + lax.rem(i + lax.rem(index, 2), count - 2), count)
        near = index + 1 - 2 * lax.rem(index, 2)
        return jnp.where(i < count - 2, far, near)

    def far_first(i):
        return others(i, me, peers)

    def owner_order(i):
        return others(i, my_term, owners)

    def launch(c):
        def one(i, carry):
            target = far_first(i)
            pick(c, target, outgoing[c], target * capacity)
            block_copy(c, target).start()
            return carry
        lax.fori_loop(0, peers - 1, one, 0)

    def sent(c):
        def one(i, carry):
            block_copy(c, far_first(i)).wait_send()
            return carry
        lax.fori_loop(0, peers - 1, one, 0)

    def sum_copy(c, owner):
        return pltpu.make_async_remote_copy(
            src_ref=sums[c].at[owner],
            dst_ref=landed[c].at[my_term],
            send_sem=sum_send_sem.at[c, owner],
            recv_sem=sum_recv_sem.at[c, my_term],
            device_id={"term": owner},
            device_id_type=MESH,
        )

    def sum_arrival(c, source):
        return pltpu.make_async_remote_copy(
            src_ref=sums[c].at[source],
            dst_ref=landed[c].at[source],
            send_sem=sum_send_sem.at[c, source],
            recv_sem=sum_recv_sem.at[c, source],
            device_id={"term": source},
            device_id_type=MESH,
        )

    pl.semaphore_wait(barrier, peers - 1 + owners - 1)
    for c in range(n_chunks):
        right_loads[c].wait()
        launch(c)
        if c == 0:
            sizes_load.start()
            partner_load.start()
            wave_load.start()
            left_load.start()
    for c in range(n_chunks):
        pick(c, me, arrived[c], me * capacity)

    sizes_load.wait()
    partner_load.wait()
    left_load.wait()
    wave_load.wait()
    row_ids = lax.broadcasted_iota(jnp.int32, (block, block), 0)
    column_ids = lax.broadcasted_iota(jnp.int32, (block, block), 1)

    def first_products(l, carry):
        own_size = sizes[me * sector_count + l]
        right_size = sizes[partner[me * sector_count + l]]
        keep = (row_ids < own_size) & (column_ids < right_size)
        masked = jnp.concatenate(
            [jnp.where(keep, wave[l, v].astype(jnp.float32), 0.0).astype(jnp.bfloat16) for v in range(vecs)], axis=1
        )
        for t in range(terms):
            product = jnp.dot(left[l, t], masked, preferred_element_type=jnp.float32).astype(jnp.bfloat16)
            for v in range(vecs):
                partial[l, v * block:(v + 1) * block, t * block:(t + 1) * block] = product[:, v * block:(v + 1) * block]
        return carry

    lax.fori_loop(0, sector_count, first_products, 0, unroll=2)

    def multiply(c, source):
        def one(r, carry):
            slot = source * capacity + r
            products[slot, 0:chunks[c], :] = lax.dot_general(
                arrived[c][slot], partial[sector_of[slot]], (((1,), (1,)), ((), ())),
                preferred_element_type=jnp.float32,
            )
            return carry
        lax.fori_loop(0, capacity, one, 0, unroll=min(capacity, 4))

    def finish(c):
        rows = pl.ds(starts[c], chunks[c])

        def wait_one(i, carry):
            sum_arrival(c, lax.rem(my_term + i, owners)).wait_recv()
            return carry
        lax.fori_loop(1, owners, wait_one, 0)

        m_ids = starts[c] + lax.broadcasted_iota(jnp.int32, (chunks[c], block), 0)
        i_ids = lax.broadcasted_iota(jnp.int32, (chunks[c], block), 1)

        def add(s, carry):
            total = out_ref[s, rows, :]
            for i in range(1, owners):
                total = total + landed[c][lax.rem(my_term + i, owners), s].astype(jnp.float32)
            sector = me * sector_count + my_term * owned + s
            keep = (m_ids < sizes[partner[sector]]) & (i_ids < sizes[sector])
            for v in range(vecs):
                out_ref[s, rows, v * block:(v + 1) * block] = jnp.where(
                    keep, total[:, v * block:(v + 1) * block], 0.0
                )
            return carry
        lax.fori_loop(0, owned, add, 0, unroll=2)

    for c in range(n_chunks):
        multiply(c, me)

        def from_source(i, carry):
            source = far_first(peers - 2 - i)
            arrival(c, source).wait_recv()
            multiply(c, source)
            return carry
        lax.fori_loop(0, peers - 1, from_source, 0)

        def for_owner(i, carry):
            owner = owner_order(i)

            def one(s, inner):
                sums[c][owner, s] = products[slot_of[owner * owned + s], 0:chunks[c], :].astype(jnp.bfloat16)
                return inner
            lax.fori_loop(0, owned, one, 0, unroll=min(owned, 4))
            sum_copy(c, owner).start()
            return carry
        lax.fori_loop(0, owners - 1, for_owner, 0)

        def for_me(s, carry):
            out_ref[s, starts[c]:starts[c] + chunks[c], :] = products[slot_of[my_term * owned + s], 0:chunks[c], :]
            return carry
        lax.fori_loop(0, owned, for_me, 0, unroll=min(owned, 4))
        if c > 0:
            finish(c - 1)
    finish(n_chunks - 1)

    for c in range(n_chunks):
        sent(c)

        def sum_sent(i, carry):
            sum_copy(c, lax.rem(my_term + i, owners)).wait_send()
            return carry
        lax.fori_loop(1, owners, sum_sent, 0)


def on_device(wavefunction, left_ops, right_ops, sector_sizes, right_partner):
    sector_count, vecs, block = wavefunction.shape[:3]
    terms = left_ops.shape[1]
    peers = lax.axis_size("sec")
    owners = lax.axis_size("term")
    own_index = lax.axis_index("sec")
    capacity = sector_count // peers
    owned = sector_count // owners
    sector_ids = jnp.arange(sector_sizes.shape[0], dtype=jnp.int32)
    source_dev = sector_ids // sector_count
    target_dev = right_partner // sector_count
    earlier = (
        (source_dev[:, None] == source_dev[None, :])
        & (target_dev[:, None] == target_dev[None, :])
        & (sector_ids[None, :] < sector_ids[:, None])
    )
    rank_within = jnp.sum(earlier.astype(jnp.int32), axis=1)
    slot_of = target_dev * capacity + rank_within
    local_slot = lax.dynamic_slice_in_dim(slot_of, own_index * sector_count, sector_count)
    slot_range = jnp.arange(sector_count, dtype=jnp.int32)
    receive_key = jnp.where(target_dev == own_index, source_dev * capacity + rank_within, -1)
    receive_index = jnp.sum(
        jnp.where(receive_key[None, :] == slot_range[:, None], (right_partner % sector_count)[None, :], 0), axis=1
    )

    slot_ids = jnp.arange(sector_count, dtype=jnp.int32)
    sector_of = jnp.sum(jnp.where(local_slot[None, :] == slot_ids[:, None], slot_ids[None, :], 0), axis=1)

    chunks = CHUNKS
    wide = terms * block
    columns = vecs * block
    n = len(chunks)
    vmem = lambda shape, dtype: pltpu.VMEM(shape, dtype)
    scratch = [
        pltpu.SMEM(sector_sizes.shape, jnp.int32),
        pltpu.SMEM(right_partner.shape, jnp.int32),
        vmem(wavefunction.shape, jnp.bfloat16),
        vmem(left_ops.shape, jnp.bfloat16),
        vmem((sector_count, columns, wide), jnp.bfloat16),
        vmem((sector_count, max(chunks), columns), jnp.float32),
    ]
    scratch += [vmem((sector_count, terms, rows, block), jnp.bfloat16) for rows in chunks]
    scratch += [vmem((sector_count, rows, wide), jnp.bfloat16) for rows in chunks]
    scratch += [vmem((sector_count, rows, wide), jnp.bfloat16) for rows in chunks]
    scratch += [vmem((owners, owned, rows, columns), jnp.bfloat16) for rows in chunks]
    scratch += [vmem((owners, owned, rows, columns), jnp.bfloat16) for rows in chunks]
    scratch += [
        pltpu.SemaphoreType.DMA((4 + n,)),
        pltpu.SemaphoreType.DMA((n, peers)),
        pltpu.SemaphoreType.DMA((n, peers)),
        pltpu.SemaphoreType.DMA((n, owners)),
        pltpu.SemaphoreType.DMA((n, owners)),
    ]
    smem = pl.BlockSpec(memory_space=pltpu.SMEM)
    anywhere = pl.BlockSpec(memory_space=pl.ANY)
    summed = pl.pallas_call(
        functools.partial(kernel, chunks),
        out_shape=jax.ShapeDtypeStruct((owned, block, columns), jnp.float32),
        in_specs=[smem, smem, smem, anywhere, anywhere, anywhere, anywhere, anywhere],
        out_specs=pl.BlockSpec(memory_space=pltpu.VMEM),
        scratch_shapes=scratch,
        compiler_params=pltpu.CompilerParams(
            collective_id=0, has_side_effects=True, vmem_limit_bytes=52 * 1024 * 1024
        ),
        cost_estimate=pl.CostEstimate(
            flops=4 * sector_count * terms * vecs * block**3, bytes_accessed=16 * 1024 * 1024, transcendentals=0
        ),
    )(receive_index, local_slot, sector_of, sector_sizes, right_partner, wavefunction, left_ops, right_ops)

    return summed.reshape(owned, block, vecs, block).transpose(0, 2, 3, 1)


def solution(mesh):
    placed = (
        P(("groups", "sec"), None, None, None),
        P(("groups", "sec"), "term", None, None),
        P(("groups", "sec"), "term", None, None),
        P("groups"),
        P("groups"),
    )
    return jax.shard_map(
        on_device,
        mesh=mesh,
        in_specs=placed,
        out_specs=P(("groups", "sec", "term"), None, None, None),
        check_vma=False,
    )
```

```python
import functools

import jax
import jax.numpy as jnp
from jax import lax
from jax.experimental import pallas as pl
from jax.experimental.pallas import tpu as pltpu
from jax.sharding import PartitionSpec as P

MESH = pl.DeviceIdType.MESH
CHUNKS = (48, 32, 32, 16)


def kernel(chunks, receive_index, slot_of, sector_of, sizes_hbm, partner_hbm, wave_hbm, left_hbm, right_hbm, out_ref,
           sizes, partner, wave, left, partial, products, *rest):
    n_chunks = len(chunks)
    right, outgoing, arrived, sums, landed = (rest[i * n_chunks:(i + 1) * n_chunks] for i in range(5))
    load_sem, send_sem, recv_sem, sum_send_sem, sum_recv_sem = rest[5 * n_chunks:]
    sector_count, vecs, block, _ = wave.shape
    terms = left.shape[1]
    peers = lax.axis_size("sec")
    owners = lax.axis_size("term")
    capacity = sector_count // peers
    owned = sector_count // owners
    me = lax.axis_index("sec")
    my_term = lax.axis_index("term")
    starts = [sum(chunks[:c]) for c in range(n_chunks)]

    right_loads = [
        pltpu.make_async_copy(right_hbm.at[:, :, pl.ds(starts[c], chunks[c])], right[c], load_sem.at[4 + c])
        for c in range(n_chunks)
    ]
    left_load = pltpu.make_async_copy(left_hbm, left, load_sem.at[0])
    wave_load = pltpu.make_async_copy(wave_hbm, wave, load_sem.at[1])
    sizes_load = pltpu.make_async_copy(sizes_hbm, sizes, load_sem.at[2])
    partner_load = pltpu.make_async_copy(partner_hbm, partner, load_sem.at[3])
    for load in right_loads:
        load.start()

    barrier = pltpu.get_barrier_semaphore()

    def greet_sec(i, carry):
        pl.semaphore_signal(barrier, inc=1, device_id={"sec": lax.rem(me + i, peers)}, device_id_type=MESH)
        return carry

    def greet_term(i, carry):
        pl.semaphore_signal(barrier, inc=1, device_id={"term": lax.rem(my_term + i, owners)}, device_id_type=MESH)
        return carry

    lax.fori_loop(1, peers, greet_sec, 0)
    lax.fori_loop(1, owners, greet_term, 0)
    def pick(c, target, into, slot_base):
        def one(r, carry):
            index = receive_index[target * capacity + r]
            for t in range(terms):
                into[slot_base + r, :, t * block:(t + 1) * block] = right[c][index, t]
            return carry
        lax.fori_loop(0, capacity, one, 0, unroll=min(capacity, 4))

    def block_copy(c, target):
        return pltpu.make_async_remote_copy(
            src_ref=outgoing[c].at[pl.ds(target * capacity, capacity)],
            dst_ref=arrived[c].at[pl.ds(me * capacity, capacity)],
            send_sem=send_sem.at[c, target],
            recv_sem=recv_sem.at[c, me],
            device_id={"sec": target},
            device_id_type=MESH,
        )

    def arrival(c, source):
        return pltpu.make_async_remote_copy(
            src_ref=outgoing[c].at[pl.ds(source * capacity, capacity)],
            dst_ref=arrived[c].at[pl.ds(source * capacity, capacity)],
            send_sem=send_sem.at[c, source],
            recv_sem=recv_sem.at[c, source],
            device_id={"sec": source},
            device_id_type=MESH,
        )

    def others(i, index, count):
        base = index - lax.rem(index, 2)
        far = lax.rem(base + 2 + lax.rem(i + lax.rem(index, 2), count - 2), count)
        near = index + 1 - 2 * lax.rem(index, 2)
        return jnp.where(i < count - 2, far, near)

    def far_first(i):
        return others(i, me, peers)

    def launch(c):
        def one(i, carry):
            target = far_first(i)
            pick(c, target, outgoing[c], target * capacity)
            block_copy(c, target).start()
            return carry
        lax.fori_loop(0, peers - 1, one, 0)

    def sent(c):
        def one(i, carry):
            block_copy(c, far_first(i)).wait_send()
            return carry
        lax.fori_loop(0, peers - 1, one, 0)

    half = owners // 2
    pair = my_term // 2
    side = lax.rem(my_term, 2)

    def sibling_copy(c):
        return pltpu.make_async_remote_copy(
            src_ref=sums[c].at[pl.ds(0, half)],
            dst_ref=landed[c].at[pl.ds(0, half)],
            send_sem=sum_send_sem.at[c, 0],
            recv_sem=sum_recv_sem.at[c, 0],
            device_id={"term": my_term + 1 - 2 * side},
            device_id_type=MESH,
        )

    def pair_copy(c, other):
        return pltpu.make_async_remote_copy(
            src_ref=sums[c].at[half + other],
            dst_ref=landed[c].at[half + pair],
            send_sem=sum_send_sem.at[c, 1 + other],
            recv_sem=sum_recv_sem.at[c, 1 + pair],
            device_id={"term": 2 * other + side},
            device_id_type=MESH,
        )

    def pair_arrival(c, other):
        return pltpu.make_async_remote_copy(
            src_ref=sums[c].at[half + other],
            dst_ref=landed[c].at[half + other],
            send_sem=sum_send_sem.at[c, 1 + other],
            recv_sem=sum_recv_sem.at[c, 1 + other],
            device_id={"term": 2 * other + side},
            device_id_type=MESH,
        )

    pl.semaphore_wait(barrier, peers - 1 + owners - 1)
    for c in range(n_chunks):
        right_loads[c].wait()
        launch(c)
        if c == 0:
            sizes_load.start()
            partner_load.start()
            wave_load.start()
            left_load.start()
    for c in range(n_chunks):
        pick(c, me, arrived[c], me * capacity)

    sizes_load.wait()
    partner_load.wait()
    left_load.wait()
    wave_load.wait()
    row_ids = lax.broadcasted_iota(jnp.int32, (block, block), 0)
    column_ids = lax.broadcasted_iota(jnp.int32, (block, block), 1)

    def first_products(l, carry):
        own_size = sizes[me * sector_count + l]
        right_size = sizes[partner[me * sector_count + l]]
        keep = (row_ids < own_size) & (column_ids < right_size)
        masked = jnp.concatenate(
            [jnp.where(keep, wave[l, v].astype(jnp.float32), 0.0).astype(jnp.bfloat16) for v in range(vecs)], axis=1
        )
        for t in range(terms):
            product = jnp.dot(left[l, t], masked, preferred_element_type=jnp.float32).astype(jnp.bfloat16)
            for v in range(vecs):
                partial[l, v * block:(v + 1) * block, t * block:(t + 1) * block] = product[:, v * block:(v + 1) * block]
        return carry

    lax.fori_loop(0, sector_count, first_products, 0, unroll=2)

    def multiply(c, source):
        def one(r, carry):
            slot = source * capacity + r
            products[slot, 0:chunks[c], :] = lax.dot_general(
                arrived[c][slot], partial[sector_of[slot]], (((1,), (1,)), ((), ())),
                preferred_element_type=jnp.float32,
            )
            return carry
        lax.fori_loop(0, capacity, one, 0, unroll=min(capacity, 4))

    def finish(c):
        rows = pl.ds(starts[c], chunks[c])

        def wait_one(i, carry):
            pair_arrival(c, lax.rem(pair + i, half)).wait_recv()
            return carry
        lax.fori_loop(1, half, wait_one, 0)
        m_ids = starts[c] + lax.broadcasted_iota(jnp.int32, (chunks[c], block), 0)
        i_ids = lax.broadcasted_iota(jnp.int32, (chunks[c], block), 1)

        def add(s, carry):
            total = out_ref[s, rows, :]
            for i in range(1, half):
                total = total + landed[c][half + lax.rem(pair + i, half), s].astype(jnp.float32)
            sector = me * sector_count + my_term * owned + s
            keep = (m_ids < sizes[partner[sector]]) & (i_ids < sizes[sector])
            for v in range(vecs):
                out_ref[s, rows, v * block:(v + 1) * block] = jnp.where(
                    keep, total[:, v * block:(v + 1) * block], 0.0
                )
            return carry
        lax.fori_loop(0, owned, add, 0, unroll=2)

    for c in range(n_chunks):
        multiply(c, me)

        def from_source(i, carry):
            source = far_first(peers - 2 - i)
            arrival(c, source).wait_recv()
            multiply(c, source)
            return carry
        lax.fori_loop(0, peers - 1, from_source, 0)

        def for_sibling(other, carry):
            owner = 2 * other + 1 - side

            def one(s, inner):
                sums[c][other, s] = products[slot_of[owner * owned + s], 0:chunks[c], :].astype(jnp.bfloat16)
                return inner
            lax.fori_loop(0, owned, one, 0, unroll=min(owned, 4))
            return carry
        lax.fori_loop(0, half, for_sibling, 0)
        sibling_copy(c).start()
        if c > 0:
            finish(c - 1)
        sibling_copy(c).wait_recv()

        def for_pair(i, carry):
            other = lax.rem(pair + i, half)
            owner = 2 * other + side

            def one(s, inner):
                own = products[slot_of[owner * owned + s], 0:chunks[c], :]
                sums[c][half + other, s] = (own + landed[c][other, s].astype(jnp.float32)).astype(jnp.bfloat16)
                return inner
            lax.fori_loop(0, owned, one, 0, unroll=min(owned, 4))
            pair_copy(c, other).start()
            return carry
        lax.fori_loop(1, half, for_pair, 0)

        def for_me(s, carry):
            own = products[slot_of[my_term * owned + s], 0:chunks[c], :]
            out_ref[s, starts[c]:starts[c] + chunks[c], :] = own + landed[c][pair, s].astype(jnp.float32)
            return carry
        lax.fori_loop(0, owned, for_me, 0, unroll=min(owned, 4))
    finish(n_chunks - 1)

    for c in range(n_chunks):
        sent(c)

        sibling_copy(c).wait_send()

        def sum_sent(i, carry):
            pair_copy(c, lax.rem(pair + i, half)).wait_send()
            return carry
        lax.fori_loop(1, half, sum_sent, 0)


def on_device(wavefunction, left_ops, right_ops, sector_sizes, right_partner):
    sector_count, vecs, block = wavefunction.shape[:3]
    terms = left_ops.shape[1]
    peers = lax.axis_size("sec")
    owners = lax.axis_size("term")
    own_index = lax.axis_index("sec")
    capacity = sector_count // peers
    owned = sector_count // owners
    sector_ids = jnp.arange(sector_sizes.shape[0], dtype=jnp.int32)
    source_dev = sector_ids // sector_count
    target_dev = right_partner // sector_count
    earlier = (
        (source_dev[:, None] == source_dev[None, :])
        & (target_dev[:, None] == target_dev[None, :])
        & (sector_ids[None, :] < sector_ids[:, None])
    )
    rank_within = jnp.sum(earlier.astype(jnp.int32), axis=1)
    slot_of = target_dev * capacity + rank_within
    local_slot = lax.dynamic_slice_in_dim(slot_of, own_index * sector_count, sector_count)
    slot_range = jnp.arange(sector_count, dtype=jnp.int32)
    receive_key = jnp.where(target_dev == own_index, source_dev * capacity + rank_within, -1)
    receive_index = jnp.sum(
        jnp.where(receive_key[None, :] == slot_range[:, None], (right_partner % sector_count)[None, :], 0), axis=1
    )

    slot_ids = jnp.arange(sector_count, dtype=jnp.int32)
    sector_of = jnp.sum(jnp.where(local_slot[None, :] == slot_ids[:, None], slot_ids[None, :], 0), axis=1)

    chunks = CHUNKS
    wide = terms * block
    columns = vecs * block
    n = len(chunks)
    vmem = lambda shape, dtype: pltpu.VMEM(shape, dtype)
    scratch = [
        pltpu.SMEM(sector_sizes.shape, jnp.int32),
        pltpu.SMEM(right_partner.shape, jnp.int32),
        vmem(wavefunction.shape, jnp.bfloat16),
        vmem(left_ops.shape, jnp.bfloat16),
        vmem((sector_count, columns, wide), jnp.bfloat16),
        vmem((sector_count, max(chunks), columns), jnp.float32),
    ]
    scratch += [vmem((sector_count, terms, rows, block), jnp.bfloat16) for rows in chunks]
    scratch += [vmem((sector_count, rows, wide), jnp.bfloat16) for rows in chunks]
    scratch += [vmem((sector_count, rows, wide), jnp.bfloat16) for rows in chunks]
    scratch += [vmem((owners, owned, rows, columns), jnp.bfloat16) for rows in chunks]
    scratch += [vmem((owners, owned, rows, columns), jnp.bfloat16) for rows in chunks]
    scratch += [
        pltpu.SemaphoreType.DMA((4 + n,)),
        pltpu.SemaphoreType.DMA((n, peers)),
        pltpu.SemaphoreType.DMA((n, peers)),
        pltpu.SemaphoreType.DMA((n, owners)),
        pltpu.SemaphoreType.DMA((n, owners)),
    ]
    smem = pl.BlockSpec(memory_space=pltpu.SMEM)
    anywhere = pl.BlockSpec(memory_space=pl.ANY)
    summed = pl.pallas_call(
        functools.partial(kernel, chunks),
        out_shape=jax.ShapeDtypeStruct((owned, block, columns), jnp.float32),
        in_specs=[smem, smem, smem, anywhere, anywhere, anywhere, anywhere, anywhere],
        out_specs=pl.BlockSpec(memory_space=pltpu.VMEM),
        scratch_shapes=scratch,
        compiler_params=pltpu.CompilerParams(
            collective_id=0, has_side_effects=True, vmem_limit_bytes=52 * 1024 * 1024
        ),
        cost_estimate=pl.CostEstimate(
            flops=4 * sector_count * terms * vecs * block**3, bytes_accessed=16 * 1024 * 1024, transcendentals=0
        ),
    )(receive_index, local_slot, sector_of, sector_sizes, right_partner, wavefunction, left_ops, right_ops)

    return summed.reshape(owned, block, vecs, block).transpose(0, 2, 3, 1)


def solution(mesh):
    placed = (
        P(("groups", "sec"), None, None, None),
        P(("groups", "sec"), "term", None, None),
        P(("groups", "sec"), "term", None, None),
        P("groups"),
        P("groups"),
    )
    return jax.shard_map(
        on_device,
        mesh=mesh,
        in_specs=placed,
        out_specs=P(("groups", "sec", "term"), None, None, None),
        check_vma=False,
    )
```
